32 devices in a mesh: groups: 2 (over y), ep: 4 (over x, core), tp: 4 (over z).
Axes of the slice: x: 2, y: 2, z: 4, core: 2. Of those that a mesh axis runs over, the one named last changes fastest.
Arguments:
- x_moe: bfloat16 [512, 7168], P(('groups', 'ep'), 'tp'), parts along dimension 0, may hold values from -6 to 6
- routes: int32 [512, 2], P(('groups', 'ep')), parts along dimension 0, may hold values from 0 to 3, all different within a row; in each aligned block of 64 rows (0 to 63, 64 to 127, ...) at most 48 rows name the same one
- router_logits: float32 [512, 2], P(('groups', 'ep')), parts along dimension 0, may hold values from -6 to 6
- w_gate: bfloat16 [4, 7168, 2048], P('ep', None, 'tp'), may hold values from -0.0625 to 0.0625
- w_up: bfloat16 [4, 7168, 2048], P('ep', None, 'tp'), may hold values from -0.0625 to 0.0625
- w_down: bfloat16 [4, 2048, 7168], P('ep', 'tp'), may hold values from -0.125 to 0.125
- q_latent: bfloat16 [512, 64, 512], P(('groups', 'ep'), 'tp'), parts along dimension 0, may hold values from -96 to 96
- q_rope: bfloat16 [512, 4096], P(('groups', 'ep'), 'tp'), parts along dimension 0, may hold values from -96 to 96
- kv_latent: bfloat16 [512, 512], P(('groups', 'ep')), parts along dimension 0, may hold values from -6 to 6
- key_rope: bfloat16 [512, 64], P(('groups', 'ep')), parts along dimension 0, may hold values from -6 to 6
- prompt_lengths: int32 [16], P('groups'), parts along dimension 0, may hold values from 1 to 128, 256 in all
Outputs:
- moe_out: bfloat16 [512, 7168], P(('groups', 'ep'), 'tp'), parts along dimension 0
- context: bfloat16 [512, 64, 512], P(('groups', 'ep'), 'tp'), parts along dimension 0
The draws below stay inside these ranges and needn't reach their ends.
There are 2 independent parts, one for each index of `groups`. The reference program is written for one: setup_inputs(seed, part) draws one part's arguments, and reference() takes and returns one part's arrays. A program takes and returns all parts, laid end to end along the dimension named above; an argument that names none is the same for every part. Nothing has to cross between parts.
Inputs may be any that keep to these rules, and one draw needn't show every extreme that they name: `routes`: in each aligned block of 64 rows (the rows of one device) no expert is named by more than 48 rows, a bound that some block reaches; every expert is named somewhere; the 2 experts of a row differ. `prompt_lengths`: the lengths sum to 256; the largest is exactly 128.
All inputs are finite; a program needn't handle non-finite values.
Results may differ from the reference program's by a relative error of at most 0.011.
Values may be sent and summed in bfloat16 or wider, within the bound.
A program may use at most 128 MiB of HBM per device.

```python
import math
import jax
import jax.numpy as jnp
import numpy as np
from jax import lax

D = 7168
FF = 2048
HEADS = 64
LATENT = 512
ROPE = 64
ROWS = 64
DOCS = 8
EXPERTS = 4
TOP = 2
CAP = 48
TOKENS = 256
N_EP = 4
N_TP = 4


def key_base(key):
    return jnp.clip(jax.random.normal(key, (TOKENS, LATENT + ROPE), jnp.float32), -6.0, 6.0)


def query_base(key):
    inner = jax.random.fold_in(key, 11)
    return jnp.clip(jax.random.normal(inner, (TOKENS, HEADS, LATENT + ROPE), jnp.float32), -6.0, 6.0)


def draw_q_latent(key, part):
    query = query_base(key)
    return query[:, :, :LATENT].astype(jnp.bfloat16)


def draw_q_rope(key, part):
    query = query_base(key)
    return query[:, :, LATENT:].reshape(TOKENS, HEADS * ROPE).astype(jnp.bfloat16)


def draw_kv_latent(key, part):
    keys = key_base(key)
    return keys[:, :LATENT].astype(jnp.bfloat16)


def draw_key_rope(key, part):
    keys = key_base(key)
    return keys[:, LATENT:].astype(jnp.bfloat16)


def shard_levels(stream_key, extent, cuts, low, high):
    level = 1.0
    for dim, blocks in cuts:
        steps = jax.random.uniform(jax.random.fold_in(jax.random.fold_in(stream_key, 6), dim), (blocks,), jnp.float32, low / len(cuts), high / len(cuts))
        level = level * jnp.repeat(jnp.exp(steps), extent[dim] // blocks).reshape((-1,) + (1,) * (len(extent) - 1 - dim))
    return level


def split_up(number_of, total, reach, skew):
    loads = [(1 << 20) // math.isqrt(grade ** skew) + 1 for grade in range(2, number_of + 1)]
    spare, given = total - reach - (number_of - 1), [1] * (number_of - 1)
    while spare > 0:
        candidates = [i for i in range(number_of - 1) if given[i] < reach]
        mass, budget = sum([loads[i] for i in candidates]), spare
        for i in candidates:
            more = min(reach - given[i], max(1, budget * loads[i] // mass), spare)
            given[i] = given[i] + more
            spare = spare - more
    return np.array([reach] + given)


def uneven(own_key, amount, total, bound, slope):
    if amount == 2:
        one = jax.random.randint(own_key, (), max(1, total - bound), min(bound, total - 1) + 1)
        return jnp.stack([one, total - one])
    sizes = jnp.asarray(split_up(amount, total, bound, slope), jnp.int32)
    twos = (amount - 1) // 2
    giver, taker = sizes[1:1 + 2 * twos:2], sizes[2:2 + 2 * twos:2]
    room = jnp.minimum(giver - 1, bound - taker)
    shifted = jax.random.randint(jax.random.fold_in(own_key, 1), (twos,), 0, 1 << 20) % (room + 1)
    sizes = sizes.at[1:1 + 2 * twos:2].set(giver - shifted).at[2:2 + 2 * twos:2].set(taker + shifted)
    return sizes[jax.random.permutation(jax.random.fold_in(own_key, 2), amount)]


def assign_block(own_key, own, number, rows, count, top, bound, skew):
    sequence = jax.random.permutation(own_key, count)
    heavy_load, ordinary = portions_of(count, rows * top, bound, skew, True), portions_of(count, rows * top, bound, skew, False)
    places = jnp.arange(count)

    def named(sizes, rotation):
        used = int((sizes > 0).sum())
        fixed = max(1, used // 4)
        shifted = fixed + (places - fixed + rotation * (used - fixed)) % max(1, count - fixed)
        return jnp.zeros((count,), jnp.int32).at[sequence[jnp.where(places < fixed, places, shifted)]].set(jnp.asarray(sizes, jnp.int32))

    sizes = jnp.where(number % 4 == 0, named(heavy_load, number // 4), named(ordinary, number - number // 4 - 1))
    mixed = jax.random.permutation(jax.random.fold_in(own, 3), count)
    donor, receiver = mixed[0:count // 2 * 2:2], mixed[1:count // 2 * 2:2]
    room = jnp.minimum(sizes[donor] - 1, bound - sizes[receiver]) // 2
    room = jnp.where((donor == sequence[0]) | (receiver == sequence[0]) | (sizes[receiver] == 0), 0, jnp.maximum(room, 0))
    shifted = jax.random.randint(jax.random.fold_in(own, 4), (count // 2,), 0, 1 << 20) % (room + 1)
    sizes = sizes.at[donor].add(-shifted).at[receiver].add(shifted)
    members = jnp.searchsorted(jnp.cumsum(sizes), jnp.arange(rows * top), side="right").astype(jnp.int32)
    grid = members.reshape(top, rows).T
    grid = grid[jax.random.permutation(jax.random.fold_in(own, 1), rows)]
    rotation = jax.random.randint(jax.random.fold_in(own, 2), (rows, 1), 0, top)
    return jnp.take_along_axis(grid, (jnp.arange(top)[None, :] + rotation) % top, axis=1)


def portions_of(number_of, total, most, slope, full):
    portions = [(1 << 20) // math.isqrt(grade ** slope) + 1 for grade in range(1, number_of + 1)]
    largest = most if full else min(most, max(-(-total // number_of), total * portions[0] // sum(portions)))
    least = 1 if total - largest >= number_of - 1 else 0
    holding, surplus = [largest] + [least] * (number_of - 1), total - largest - least * (number_of - 1)
    while surplus > 0:
        movable = [i for i in range(1, number_of) if holding[i] < largest] or [i for i in range(1, number_of) if holding[i] < most]
        pool, budget = sum([portions[i] for i in movable]), surplus
        for i in movable:
            more = min(most - holding[i], max(1, budget * portions[i] // pool), surplus)
            holding[i] = holding[i] + more
            surplus = surplus - more
    return np.array(holding)


def centred(stream_key, shape, scale, limit, cuts=(), held_as=jnp.bfloat16):
    entries = jax.random.normal(stream_key, shape, jnp.float32) * scale
    if len(cuts) > 0:
        entries = shard_levels(stream_key, shape, cuts, -0.22, 0.18) * entries
    return jnp.clip(entries, min=-limit, max=limit).astype(held_as)


def setup_inputs(seed: int = 0, part: int = 0) -> dict:
    key_list = jax.random.split(jax.random.key(seed), 12)
    part_keys = jax.random.split(jax.random.fold_in(key_list[11], part), 12)
    x_moe = centred(part_keys[0], (TOKENS, D), 1.0, 6.0, ((0, 4), (1, 4)))
    routes_keys = jax.random.split(jax.random.fold_in(part_keys[1], 1), TOKENS // ROWS)
    routes_turns = jax.random.permutation(jax.random.fold_in(part_keys[1], 3), TOKENS // ROWS)
    routes = jax.vmap(lambda own, number: assign_block(jax.random.fold_in(part_keys[1], 2), own, number, ROWS, EXPERTS, TOP, CAP, 1))(routes_keys, routes_turns).reshape((TOKENS, TOP))
    router_logits = centred(part_keys[2], (TOKENS, TOP), 1.5, 6.0, ((0, 4),), jnp.float32)
    w_gate = centred(key_list[3], (EXPERTS, D, FF), D ** -0.5, 0.0625, ((0, 4), (2, 4)))
    w_up = centred(key_list[4], (EXPERTS, D, FF), D ** -0.5, 0.0625, ((0, 4), (2, 4)))
    w_down = centred(key_list[5], (EXPERTS, FF, D), FF ** -0.5, 0.125, ((0, 4), (1, 4)))
    q_latent = draw_q_latent(jax.random.fold_in(jax.random.fold_in(key_list[11], part), 71), part)
    q_rope = draw_q_rope(jax.random.fold_in(jax.random.fold_in(key_list[11], part), 71), part)
    kv_latent = draw_kv_latent(jax.random.fold_in(jax.random.fold_in(key_list[11], part), 71), part)
    key_rope = draw_key_rope(jax.random.fold_in(jax.random.fold_in(key_list[11], part), 71), part)
    prompt_lengths = uneven(part_keys[10], DOCS, TOKENS, TOKENS // 2, 2).astype(jnp.int32)
    return dict(x_moe=x_moe, routes=routes, router_logits=router_logits, w_gate=w_gate, w_up=w_up, w_down=w_down, q_latent=q_latent, q_rope=q_rope, kv_latent=kv_latent, key_rope=key_rope, prompt_lengths=prompt_lengths)


score_scale = 192.0 ** -0.5
route_scale = 2.5


def prompt_of(lengths, positions):
    ends = jnp.cumsum(lengths.astype(jnp.int32))
    return jnp.sum((positions[:, None] >= ends[None, :]).astype(jnp.int32), axis=1)


def reference(x_moe, routes, router_logits, w_gate, w_up, w_down, q_latent, q_rope, kv_latent, key_rope, prompt_lengths):
    tokens = x_moe.shape[0]
    slots = N_EP * CAP
    flat = routes.reshape(-1).astype(jnp.int32)
    onehot = (flat[:, None] == jnp.arange(EXPERTS, dtype=jnp.int32)[None, :]).astype(jnp.int32)
    rank = jnp.sum((jnp.cumsum(onehot, axis=0) - onehot) * onehot, axis=1)
    dest = flat * slots + rank
    owner = jnp.repeat(jnp.arange(tokens, dtype=jnp.int32), TOP)
    table = jnp.zeros((EXPERTS * slots,), jnp.int32).at[dest].set(owner).reshape(EXPERTS, slots)

    def expert(args):
        picks, wg, wu, wd = args
        rows = x_moe[picks]
        gate_act = jnp.dot(rows, wg, preferred_element_type=jnp.float32)
        up_act = jnp.dot(rows, wu, preferred_element_type=jnp.float32)
        hidden = (jax.nn.silu(gate_act) * up_act).astype(jnp.bfloat16)
        parts = jnp.einsum("sgf,gfd->gsd", hidden.reshape(slots, N_TP, FF // N_TP).astype(jnp.float32),
                           wd.reshape(N_TP, FF // N_TP, D).astype(jnp.float32), precision=lax.Precision.HIGHEST)
        parts = lax.optimization_barrier(parts.astype(jnp.bfloat16)).astype(jnp.float32)
        return jnp.sum(parts, axis=0).astype(jnp.bfloat16)

    outs = lax.map(expert, (table, w_gate, w_up, w_down)).reshape(EXPERTS * slots, D)
    picked = outs[dest].astype(jnp.float32).reshape(tokens, TOP, D)
    probs = jax.nn.sigmoid(router_logits)
    gates = route_scale * probs / jnp.sum(probs, axis=1, keepdims=True)
    moe_out = jnp.sum(gates[:, :, None] * picked, axis=1).astype(jnp.bfloat16)

    positions = jnp.arange(tokens, dtype=jnp.int32)
    prompts = prompt_of(prompt_lengths, positions)
    visible = (prompts[:, None] == prompts[None, :]) & (positions[None, :] <= positions[:, None])
    rope_q = q_rope.reshape(tokens, HEADS, ROPE)

    def head(args):
        lat, rot = args
        scores = (jnp.dot(lat, kv_latent.T, preferred_element_type=jnp.float32)
                  + jnp.dot(rot, key_rope.T, preferred_element_type=jnp.float32)) * score_scale
        masked = jnp.where(visible, scores, -1e30)
        top = jnp.max(masked, axis=1, keepdims=True)
        weights = jnp.where(visible, jnp.exp(masked - top), 0.0)
        total = jnp.sum(weights, axis=1, keepdims=True)
        ctx = jnp.dot(weights.astype(jnp.bfloat16), kv_latent, preferred_element_type=jnp.float32) / total
        return ctx.astype(jnp.bfloat16)

    ctx = lax.map(head, (jnp.swapaxes(q_latent, 0, 1), jnp.swapaxes(rope_q, 0, 1)))
    return moe_out, jnp.swapaxes(ctx, 0, 1)
```

```python
import functools

import jax
import jax.numpy as jnp
from jax import lax
from jax.experimental import pallas as pl
from jax.experimental.pallas import tpu as pltpu
from jax.sharding import PartitionSpec as P

MESH = pl.DeviceIdType.MESH
score_scale = 192.0 ** (-0.5)
route_scale = 2.5
CORES = 2


def prompt_of(lengths, positions):
    ends = jnp.cumsum(lengths)
    return jnp.sum((positions[:, None] >= ends[None, :]).astype(jnp.int32), axis=1)


def kernel(
    n_ep,
    n_tp,
    x_ref,
    gt_ref,
    ql_ref,
    qr_ref,
    kv_ref,
    kr_ref,
    bias_ref,
    wg_ref,
    wu_ref,
    wd_ref,
    moe_ref,
    ctx_ref,
    xall,
    gall,
    keys,
    rots,
    wg,
    wu,
    wd,
    acc_g,
    acc_u,
    hid,
    gcol,
    part,
    from_core,
    from_x,
    from_z,
    zsend,
    w_sem,
    small_send,
    small_recv,
    zg_send,
    zg_recv,
    xg_send,
    xg_recv,
    cg_send,
    cg_recv,
    cr_send,
    cr_recv,
    xr_send,
    xr_recv,
    zr_send,
    zr_recv,
):
    n_x = n_ep // CORES
    me = lax.axis_index("ep")
    z = lax.axis_index("tp")
    core = me % CORES
    xx = me // CORES
    other = me + 1 - 2 * core
    rows, width = x_ref.shape
    hidden_units = wg.shape[1]
    tokens = n_ep * rows

    def remote(src, dst, send, recv, ep=None, tp=None):
        where = {}
        if ep is not None:
            where["ep"] = ep
        if tp is not None:
            where["tp"] = tp
        return pltpu.make_async_remote_copy(
            src_ref=src, dst_ref=dst, send_sem=send, recv_sem=recv, device_id=where, device_id_type=MESH
        )

    def ep_peer(step):
        return lax.rem(me + step, n_ep)

    def x_of(step):
        return lax.rem(xx + step, n_x)

    def w_copies(b):
        span = pl.ds(pl.multiple_of(b * width, width), width)
        return (
            pltpu.make_async_copy(wg_ref.at[0, span, :], wg.at[span, :], w_sem.at[0, b]),
            pltpu.make_async_copy(wu_ref.at[0, span, :], wu.at[span, :], w_sem.at[1, b]),
            pltpu.make_async_copy(
                wd_ref.at[0, :, pl.ds(pl.multiple_of(b * width, 128), width)], wd.at[b], w_sem.at[2, b]
            ),
        )

    def sides(d):
        if d == 0:
            return [(None, z)]
        return [(z >= d, z - d), (z + d < n_tp, z + d)]

    def on(cond, fn):
        if cond is None:
            fn()
        else:
            pl.when(cond)(fn)

    def start_w(d, which):
        for cond, b in sides(d):

            def go(b=b):
                for i in which:
                    w_copies(b)[i].start()

            on(cond, go)

    barrier = pltpu.get_barrier_semaphore()
    for s in range(1, n_ep):
        pl.semaphore_signal(barrier, inc=1, device_id={"ep": ep_peer(s)}, device_id_type=MESH)

    @pl.when(z > 0)
    def _():
        pl.semaphore_signal(barrier, inc=1, device_id={"tp": z - 1}, device_id_type=MESH)

    @pl.when(z < n_tp - 1)
    def _():
        pl.semaphore_signal(barrier, inc=1, device_id={"tp": z + 1}, device_id_type=MESH)

    for d in range(n_tp):
        start_w(d, (0, 1))
    for d in range(n_tp - 1, -1, -1):
        start_w(d, (2,))

    edge = (z == 0) | (z == n_tp - 1)

    @pl.when(edge)
    def _():
        pl.semaphore_wait(barrier, n_ep)

    @pl.when(jnp.logical_not(edge))
    def _():
        pl.semaphore_wait(barrier, n_ep + 1)

    def gate_copy(s):
        return remote(gt_ref, gall.at[me], small_send.at[0, s], small_recv.at[0, s], ep=ep_peer(s))

    def gate_arrival(s):
        src = lax.rem(me + n_ep - s, n_ep)
        return remote(gt_ref, gall.at[src], small_send.at[0, s], small_recv.at[0, s], ep=ep_peer(s))

    def key_x(s):
        dst = x_of(s) * CORES + core
        return (
            remote(kv_ref, keys.at[me], small_send.at[1, s], small_recv.at[1, s], ep=dst),
            remote(kr_ref, rots.at[me], small_send.at[2, s], small_recv.at[2, s], ep=dst),
        )

    def key_core(s, owner, own):
        src_kv = kv_ref if own else keys.at[owner]
        src_kr = kr_ref if own else rots.at[owner]
        return (
            remote(src_kv, keys.at[owner], small_send.at[3, s], small_recv.at[3, s], ep=other),
            remote(src_kr, rots.at[owner], small_send.at[4, s], small_recv.at[4, s], ep=other),
        )

    for s in range(1, n_x):
        for c in key_x(s):
            c.start()
    for c in key_core(0, me, True):
        c.start()
    for s in range(1, n_ep):
        gate_copy(s).start()

    def zg(direction, b, own):
        to = z + 1 if direction == 0 else z - 1
        return remote(
            x_ref if own else xall.at[b, me],
            xall.at[b, me],
            zg_send.at[direction, b],
            zg_recv.at[direction, b],
            tp=to,
        )

    def xg(s, b, own):
        return remote(
            x_ref if own else xall.at[b, me],
            xall.at[b, me],
            xg_send.at[s, b],
            xg_recv.at[s, b],
            ep=x_of(s) * CORES + core,
        )

    def xg_in(s, b):
        src = lax.rem(xx + n_x - s, n_x) * CORES + core
        return remote(xall.at[b, src], xall.at[b, src], xg_send.at[s, b], xg_recv.at[s, b], ep=src), src

    def cg(s, b, owner, own):
        return remote(
            x_ref if own else xall.at[b, owner],
            xall.at[b, owner],
            cg_send.at[s, b],
            cg_recv.at[s, b],
            ep=other,
        )

    def cg_in(s, b):
        src = lax.rem(xx + n_x - s, n_x) * CORES + 1 - core
        return remote(xall.at[b, src], xall.at[b, src], cg_send.at[s, b], cg_recv.at[s, b], ep=other)

    def spread(b, own):
        for s in range(1, n_x):
            xg(s, b, own).start()
        cg(0, b, me, own).start()

    @pl.when(z < n_tp - 1)
    def _():
        zg(0, z, True).start()

    @pl.when(z > 0)
    def _():
        zg(1, z, True).start()

    spread(z, True)
    xall[z, me] = x_ref[...]
    keys[me] = kv_ref[...]
    rots[me] = kr_ref[...]
    gall[me] = gt_ref[...]
    acc_g[...] = jnp.zeros_like(acc_g)
    acc_u[...] = jnp.zeros_like(acc_u)

    for s in range(1, n_x):
        src = lax.rem(xx + n_x - s, n_x) * CORES + core
        for c in key_x(s):
            c.wait_recv()
        for c in key_core(s, src, False):
            c.start()
    for s in range(n_x):
        src = lax.rem(xx + n_x - s, n_x) * CORES + 1 - core
        for c in key_core(s, src, False):
            c.wait_recv()

    heads = ql_ref.shape[0] // rows
    block_tokens = 16
    block = block_tokens * heads

    def attend(i, carry):
        at = pl.multiple_of(i * block, block)
        all_keys = keys[...].reshape(tokens, keys.shape[2])
        all_rots = rots[...].reshape(tokens, rots.shape[2])
        dims = (((1,), (1,)), ((), ()))
        scores = lax.dot_general(
            ql_ref[pl.ds(at, block), :], all_keys, dims, preferred_element_type=jnp.float32
        )
        scores += lax.dot_general(
            qr_ref[pl.ds(at, block), :], all_rots, dims, preferred_element_type=jnp.float32
        )
        bias = bias_ref[pl.ds(pl.multiple_of(i * block_tokens, block_tokens), block_tokens), :]
        bias = jnp.broadcast_to(bias[:, None, :], (block_tokens, heads, tokens)).reshape(block, tokens)
        masked = jnp.where(bias < 0.0, -1e30, scores * score_scale)
        top = jnp.max(masked, axis=1, keepdims=True)
        weights = jnp.where(bias < 0.0, 0.0, jnp.exp(masked - top))
        total = jnp.sum(weights, axis=1, keepdims=True)
        out = jnp.dot(weights.astype(jnp.bfloat16), all_keys, preferred_element_type=jnp.float32)
        ctx_ref[pl.ds(at, block), :] = (out / total).astype(jnp.bfloat16)
        return carry

    lax.fori_loop(0, rows // block_tokens, attend, 0)

    tile = 256

    def multiply(b):
        for i in (0, 1):
            w_copies(b)[i].wait()
        span = pl.ds(pl.multiple_of(b * width, width), width)

        def column(j, carry):
            cols = pl.ds(pl.multiple_of(j * tile, tile), tile)
            x = xall[b].reshape(tokens, width)
            acc_g[:, cols] += jnp.dot(x, wg[span, cols], preferred_element_type=jnp.float32)
            acc_u[:, cols] += jnp.dot(x, wu[span, cols], preferred_element_type=jnp.float32)
            return carry

        lax.fori_loop(0, hidden_units // tile, column, 0)

    def process(b):
        for s in range(1, n_x):
            arrival, src = xg_in(s, b)
            arrival.wait_recv()
            cg(s, b, src, False).start()
        for s in range(n_x):
            cg_in(s, b).wait_recv()
        multiply(b)

    for d in range(1, n_tp + 1):
        if d < n_tp:

            @pl.when(z >= d)
            def _():
                b = z - d
                zg(0, b, False).wait_recv()

                @pl.when(z < n_tp - 1)
                def _():
                    zg(0, b, False).start()

                spread(b, False)

            @pl.when(z + d < n_tp)
            def _():
                b = z + d
                zg(1, b, False).wait_recv()

                @pl.when(z > 0)
                def _():
                    zg(1, b, False).start()

                spread(b, False)

        for cond, b in sides(d - 1):
            on(cond, functools.partial(process, b))

    gate_act = acc_g[...]
    hid[...] = (gate_act / (1.0 + jnp.exp(-gate_act)) * acc_u[...]).astype(jnp.bfloat16)
    for s in range(1, n_ep):
        gate_arrival(s).wait_recv()
    experts = gall.shape[1]
    mine = lax.broadcasted_iota(jnp.int32, (experts, 128), 0) == me

    for e in range(n_ep):
        row = jnp.sum(jnp.where(mine, gall[e], 0.0), axis=0, keepdims=True)
        square = jnp.broadcast_to(row, (128, 128)).T
        gcol[e * rows : (e + 1) * rows, :] = square[:rows, :]

    def cr(s, b):
        owner = x_of(s) * CORES + 1 - core
        return remote(part.at[b, owner], from_core.at[s, b], cr_send.at[s, b], cr_recv.at[s, b], ep=other)

    def xr(s, b):
        dst = x_of(s) * CORES + core
        return remote(part.at[b, dst], from_x.at[s - 1, b], xr_send.at[s, b], xr_recv.at[s, b], ep=dst)

    down_tile = 256 if width % 256 == 0 else 128

    def down(b):
        w_copies(b)[2].wait()

        def column(j, carry):
            cols = pl.ds(pl.multiple_of(j * down_tile, down_tile), down_tile)
            out = jnp.dot(hid[...], wd[b, :, cols], preferred_element_type=jnp.float32)
            out = (out * gcol[:, :1]).astype(jnp.bfloat16)
            part[b, :, :, cols] = out.reshape(n_ep, rows, down_tile)
            return carry

        lax.fori_loop(0, width // down_tile, column, 0)
        for s in range(1, n_x):
            cr(s, b).start()
        cr(0, b).start()

    def over_x(b):
        for s in range(1, n_x):
            dst = x_of(s) * CORES + core
            cr(s, b).wait_recv()
            part[b, dst] = (
                part[b, dst].astype(jnp.float32) + from_core[s, b].astype(jnp.float32)
            ).astype(jnp.bfloat16)
            xr(s, b).start()

    for d in range(n_tp - 1, -2, -1):
        if d >= 0:
            for cond, b in sides(d):
                on(cond, functools.partial(down, b))
        if d + 1 < n_tp:
            for cond, b in sides(d + 1):
                on(cond, functools.partial(over_x, b))

    def zr(direction, b):
        to = z + 1 if direction == 0 else z - 1
        return remote(
            zsend.at[b], from_z.at[direction, b], zr_send.at[b], zr_recv.at[direction, b], tp=to
        )

    def chip_sum(b):
        cr(0, b).wait_recv()
        total = part[b, me].astype(jnp.float32) + from_core[0, b].astype(jnp.float32)
        for s in range(1, n_x):
            xr(s, b).wait_recv()
            total += from_x[s - 1, b].astype(jnp.float32)
        return total

    def along(direction, b, first):
        @pl.when(first)
        def _():
            zsend[b] = chip_sum(b).astype(jnp.bfloat16)

        @pl.when(jnp.logical_not(first))
        def _():
            zr(direction, b).wait_recv()
            zsend[b] = (chip_sum(b) + from_z[direction, b].astype(jnp.float32)).astype(jnp.bfloat16)

        zr(direction, b).start()

    for d in range(n_tp - 1, 0, -1):
        pl.when(z >= d)(functools.partial(along, 1, z - d, z == n_tp - 1))
        pl.when(z + d < n_tp)(functools.partial(along, 0, z + d, z == 0))

    zsum = acc_final = chip_sum(z)

    @pl.when(z == 0)
    def _():
        zr(1, z).wait_recv()
        moe_ref[...] = (acc_final + from_z[1, z].astype(jnp.float32)).astype(jnp.bfloat16)

    @pl.when(z == n_tp - 1)
    def _():
        zr(0, z).wait_recv()
        moe_ref[...] = (acc_final + from_z[0, z].astype(jnp.float32)).astype(jnp.bfloat16)

    @pl.when((z > 0) & (z < n_tp - 1))
    def _():
        zr(0, z).wait_recv()
        zr(1, z).wait_recv()
        moe_ref[...] = (
            zsum + from_z[0, z].astype(jnp.float32) + from_z[1, z].astype(jnp.float32)
        ).astype(jnp.bfloat16)

    for s in range(1, n_ep):
        gate_copy(s).wait_send()
    for s in range(1, n_x):
        for c in key_x(s):
            c.wait_send()
    for s in range(n_x):
        for c in key_core(s, me, True):
            c.wait_send()

    def drain(b, own):
        for s in range(1, n_x):
            xg(s, b, own).wait_send()
            xr(s, b).wait_send()
        for s in range(n_x):
            cg(s, b, me, False).wait_send()
            cr(s, b).wait_send()

    for d in range(n_tp):
        for cond, b in sides(d):
            on(cond, functools.partial(drain, b, d == 0))

    @pl.when(z < n_tp - 1)
    def _():
        zg(0, z, True).wait_send()

    @pl.when(z > 0)
    def _():
        zg(1, z, True).wait_send()

    for d in range(1, n_tp):

        @pl.when((z >= d) & (z < n_tp - 1))
        def _():
            zg(0, z - d, False).wait_send()

        @pl.when((z + d < n_tp) & (z > 0))
        def _():
            zg(1, z + d, False).wait_send()

        @pl.when(z >= d)
        def _():
            zr(1, z - d).wait_send()

        @pl.when(z + d < n_tp)
        def _():
            zr(0, z + d).wait_send()


def body(
    x_moe,
    routes,
    router_logits,
    w_gate,
    w_up,
    w_down,
    q_latent,
    q_rope,
    kv_latent,
    key_rope,
    prompt_lengths,
):
    n_ep = lax.axis_size("ep")
    n_tp = lax.axis_size("tp")
    n_x = n_ep // CORES
    rows, width = x_moe.shape
    _, heads, latent = q_latent.shape
    rope = key_rope.shape[1]
    units = w_gate.shape[2]
    tokens = n_ep * rows
    experts = max(8, n_ep)

    probs = jax.nn.sigmoid(router_logits)
    gates = route_scale * probs / jnp.sum(probs, axis=1, keepdims=True)
    names = jnp.arange(experts, dtype=jnp.int32)[:, None, None]
    table = jnp.sum(jnp.where(routes[None] == names, gates[None], 0.0), axis=2)
    table = jnp.pad(table, ((0, 0), (0, 128 - rows)))

    q_pos = lax.axis_index("ep") * rows + jnp.arange(rows, dtype=jnp.int32)
    k_pos = jnp.arange(tokens, dtype=jnp.int32)
    q_prompt = prompt_of(prompt_lengths, q_pos)
    k_prompt = prompt_of(prompt_lengths, k_pos)
    visible = (q_prompt[:, None] == k_prompt[None, :]) & (k_pos[None, :] <= q_pos[:, None])
    bias = jnp.where(visible, 0.0, -1.0).astype(jnp.float32)

    vmem = pl.BlockSpec(memory_space=pltpu.VMEM)
    hbm = pl.BlockSpec(memory_space=pl.ANY)
    bf16, f32 = jnp.bfloat16, jnp.float32
    dma = pltpu.SemaphoreType.DMA
    moe, ctx = pl.pallas_call(
        functools.partial(kernel, n_ep, n_tp),
        out_shape=(
            jax.ShapeDtypeStruct((rows, width), bf16),
            jax.ShapeDtypeStruct((rows * heads, latent), bf16),
        ),
        in_specs=[vmem] * 7 + [hbm] * 3,
        out_specs=(vmem, vmem),
        scratch_shapes=[
            pltpu.VMEM((n_tp, n_ep, rows, width), bf16),
            pltpu.VMEM((n_ep, experts, 128), f32),
            pltpu.VMEM((n_ep, rows, latent), bf16),
            pltpu.VMEM((n_ep, rows, rope), bf16),
            pltpu.VMEM((n_tp * width, units), bf16),
            pltpu.VMEM((n_tp * width, units), bf16),
            pltpu.VMEM((n_tp, units, width), bf16),
            pltpu.VMEM((tokens, units), f32),
            pltpu.VMEM((tokens, units), f32),
            pltpu.VMEM((tokens, units), bf16),
            pltpu.VMEM((tokens, 128), f32),
            pltpu.VMEM((n_tp, n_ep, rows, width), bf16),
            pltpu.VMEM((n_x, n_tp, rows, width), bf16),
            pltpu.VMEM((n_x - 1, n_tp, rows, width), bf16),
            pltpu.VMEM((2, n_tp, rows, width), bf16),
            pltpu.VMEM((n_tp, rows, width), bf16),
            dma((3, n_tp)),
            dma((5, n_ep)),
            dma((5, n_ep)),
            dma((2, n_tp)),
            dma((2, n_tp)),
            dma((n_x, n_tp)),
            dma((n_x, n_tp)),
            dma((n_x, n_tp)),
            dma((n_x, n_tp)),
            dma((n_x, n_tp)),
            dma((n_x, n_tp)),
            dma((n_x, n_tp)),
            dma((n_x, n_tp)),
            dma((n_tp,)),
            dma((2, n_tp)),
        ],
        compiler_params=pltpu.CompilerParams(
            collective_id=0, has_side_effects=True, vmem_limit_bytes=62 * 1024 * 1024
        ),
        name="layer",
    )(
        x_moe,
        table,
        q_latent.reshape(rows * heads, latent),
        q_rope.reshape(rows * heads, rope),
        kv_latent,
        key_rope,
        bias,
        w_gate,
        w_up,
        w_down,
    )
    return moe, ctx.reshape(rows, heads, latent)


def solution(mesh):
    in_specs = (
        P(("groups", "ep"), "tp"),
        P(("groups", "ep"), None),
        P(("groups", "ep"), None),
        P("ep", None, "tp"),
        P("ep", None, "tp"),
        P("ep", "tp", None),
        P(("groups", "ep"), "tp", None),
        P(("groups", "ep"), "tp"),
        P(("groups", "ep"), None),
        P(("groups", "ep"), None),
        P("groups"),
    )
    out_specs = (P(("groups", "ep"), "tp"), P(("groups", "ep"), "tp", None))
    return jax.shard_map(body, mesh=mesh, in_specs=in_specs, out_specs=out_specs, check_vma=False)
```

```python
import functools

import jax
import jax.numpy as jnp
from jax import lax
from jax.experimental import pallas as pl
from jax.experimental.pallas import tpu as pltpu
from jax.sharding import PartitionSpec as P

MESH = pl.DeviceIdType.MESH
score_scale = 192.0 ** (-0.5)
route_scale = 2.5
CORES = 2


def kernel(
    n_ep,
    n_tp,
    x_ref,
    routes_ref,
    logits_ref,
    ql_ref,
    qr_ref,
    kv_ref,
    kr_ref,
    lengths_ref,
    wg_ref,
    wu_ref,
    wd_ref,
    moe_ref,
    ctx_ref,
    xall,
    gt_ref,
    gall,
    rope_keys,
    hidden_from,
    keys,
    rots,
    wg,
    wu,
    wd,
    acc_g,
    acc_u,
    hid,
    gcol,
    part,
    from_core,
    from_x,
    from_z,
    w_sem,
    small_send,
    small_recv,
    zg_send,
    zg_recv,
    xg_send,
    xg_recv,
    cg_send,
    cg_recv,
    cr_send,
    cr_recv,
    xr_send,
    xr_recv,
    zr_send,
    zr_recv,
):
    n_x = n_ep // CORES
    me = lax.axis_index("ep")
    z = lax.axis_index("tp")
    core = me % CORES
    xx = me // CORES
    other = me + 1 - 2 * core
    rows, width = x_ref.shape
    hidden_units = wg.shape[1]
    tokens = n_ep * rows

    def remote(src, dst, send, recv, ep=None, tp=None):
        where = {}
        if ep is not None:
            where["ep"] = ep
        if tp is not None:
            where["tp"] = tp
        return pltpu.make_async_remote_copy(
            src_ref=src, dst_ref=dst, send_sem=send, recv_sem=recv, device_id=where, device_id_type=MESH
        )

    def ep_peer(step):
        return lax.rem(me + step, n_ep)

    def x_of(step):
        return lax.rem(xx + step, n_x)

    def w_copies(b):
        span = pl.ds(pl.multiple_of(b * width, width), width)
        return (
            pltpu.make_async_copy(wg_ref.at[0, span, :], wg.at[span, :], w_sem.at[0, b]),
            pltpu.make_async_copy(wu_ref.at[0, span, :], wu.at[span, :], w_sem.at[1, b]),
            pltpu.make_async_copy(
                wd_ref.at[0, :, pl.ds(pl.multiple_of(b * width, 128), width)], wd.at[b], w_sem.at[2, b]
            ),
        )

    def sides(d):
        if d == 0:
            return [(None, z)]
        return [(z >= d, z - d), (z + d < n_tp, z + d)]

    def on(cond, fn):
        if cond is None:
            fn()
        else:
            pl.when(cond)(fn)

    def start_w(d, which):
        for cond, b in sides(d):

            def go(b=b):
                for i in which:
                    w_copies(b)[i].start()

            on(cond, go)

    barrier = pltpu.get_barrier_semaphore()
    for s in range(1, n_ep):
        pl.semaphore_signal(barrier, inc=1, device_id={"ep": ep_peer(s)}, device_id_type=MESH)

    @pl.when(z > 0)
    def _():
        pl.semaphore_signal(barrier, inc=1, device_id={"tp": z - 1}, device_id_type=MESH)

    @pl.when(z < n_tp - 1)
    def _():
        pl.semaphore_signal(barrier, inc=1, device_id={"tp": z + 1}, device_id_type=MESH)

    probs = 1.0 / (1.0 + jnp.exp(-logits_ref[...]))
    gates = route_scale * probs / jnp.sum(probs, axis=1, keepdims=True)
    lanes = lax.broadcasted_iota(jnp.int32, (rows, 128), 1)
    table = jnp.zeros((rows, 128), jnp.float32)
    for k in range(routes_ref.shape[1]):
        table += jnp.where(routes_ref[:, k : k + 1] == lanes, gates[:, k : k + 1], 0.0)
    square = jnp.concatenate([table, jnp.zeros((128 - rows, 128), jnp.float32)], axis=0)
    gt_ref[...] = square.T[: gt_ref.shape[0], :]

    edge = (z == 0) | (z == n_tp - 1)

    @pl.when(edge)
    def _():
        pl.semaphore_wait(barrier, n_ep)

    @pl.when(jnp.logical_not(edge))
    def _():
        pl.semaphore_wait(barrier, n_ep + 1)

    def gate_copy(s):
        return remote(gt_ref, gall.at[me], small_send.at[0, s], small_recv.at[0, s], ep=ep_peer(s))

    def gate_arrival(s):
        src = lax.rem(me + n_ep - s, n_ep)
        return remote(gt_ref, gall.at[src], small_send.at[0, s], small_recv.at[0, s], ep=ep_peer(s))

    def key_x(s):
        dst = x_of(s) * CORES + core
        return (
            remote(kv_ref, keys.at[me], small_send.at[1, s], small_recv.at[1, s], ep=dst),
            remote(kr_ref, rots.at[me], small_send.at[2, s], small_recv.at[2, s], ep=dst),
        )

    def key_core(s, owner, own):
        src_kv = kv_ref if own else keys.at[owner]
        src_kr = kr_ref if own else rots.at[owner]
        return (
            remote(src_kv, keys.at[owner], small_send.at[3, s], small_recv.at[3, s], ep=other),
            remote(src_kr, rots.at[owner], small_send.at[4, s], small_recv.at[4, s], ep=other),
        )

    def zg(direction, b, own):
        to = z + 1 if direction == 0 else z - 1
        return remote(
            x_ref if own else xall.at[b, me],
            xall.at[b, me],
            zg_send.at[direction, b],
            zg_recv.at[direction, b],
            tp=to,
        )

    def xg(s, b, own):
        return remote(
            x_ref if own else xall.at[b, me],
            xall.at[b, me],
            xg_send.at[s, b],
            xg_recv.at[s, b],
            ep=x_of(s) * CORES + core,
        )

    def xg_in(s, b):
        src = lax.rem(xx + n_x - s, n_x) * CORES + core
        return remote(xall.at[b, src], xall.at[b, src], xg_send.at[s, b], xg_recv.at[s, b], ep=src), src

    def cg(s, b, owner, own):
        return remote(
            x_ref if own else xall.at[b, owner],
            xall.at[b, owner],
            cg_send.at[s, b],
            cg_recv.at[s, b],
            ep=other,
        )

    def cg_in(s, b):
        src = lax.rem(xx + n_x - s, n_x) * CORES + 1 - core
        return remote(xall.at[b, src], xall.at[b, src], cg_send.at[s, b], cg_recv.at[s, b], ep=other)

    def spread(b, own):
        for s in range(1, n_x):
            xg(s, b, own).start()
        cg(0, b, me, own).start()

    @pl.when(z < n_tp - 1)
    def _():
        zg(0, z, True).start()

    @pl.when(z > 0)
    def _():
        zg(1, z, True).start()

    spread(z, True)
    for s in range(1, n_x):
        for c in key_x(s):
            c.start()
    for c in key_core(0, me, True):
        c.start()
    for s in range(1, n_ep):
        gate_copy(s).start()

    for d in range(n_tp):
        start_w(d, (0, 1))
    xall[z, me] = x_ref[...]
    keys[me] = kv_ref[...]
    rots[me] = kr_ref[...]
    gall[me] = gt_ref[...]
    acc_g[...] = jnp.zeros_like(acc_g)
    acc_u[...] = jnp.zeros_like(acc_u)


    tile = 256

    def multiply(b):
        for i in (0, 1):
            w_copies(b)[i].wait()
        span = pl.ds(pl.multiple_of(b * width, width), width)

        def column(j, carry):
            cols = pl.ds(pl.multiple_of(j * tile, tile), tile)
            x = xall[b].reshape(tokens, width)
            acc_g[:, cols] += jnp.dot(x, wg[span, cols], preferred_element_type=jnp.float32)
            acc_u[:, cols] += jnp.dot(x, wu[span, cols], preferred_element_type=jnp.float32)
            return carry

        lax.fori_loop(0, hidden_units // tile, column, 0)

    def process(b):
        for s in range(1, n_x):
            arrival, src = xg_in(s, b)
            arrival.wait_recv()
            cg(s, b, src, False).start()
        for s in range(n_x):
            cg_in(s, b).wait_recv()
        multiply(b)

    for d in range(1, n_tp + 1):
        if d < n_tp:

            @pl.when(z >= d)
            def _():
                b = z - d
                zg(0, b, False).wait_recv()

                @pl.when(z < n_tp - 1)
                def _():
                    zg(0, b, False).start()

                spread(b, False)

            @pl.when(z + d < n_tp)
            def _():
                b = z + d
                zg(1, b, False).wait_recv()

                @pl.when(z > 0)
                def _():
                    zg(1, b, False).start()

                spread(b, False)

        if d == 2:
            for far in range(n_tp - 1, -1, -1):
                start_w(far, (2,))
            for s in range(1, n_x):
                src = lax.rem(xx + n_x - s, n_x) * CORES + core
                for c in key_x(s):
                    c.wait_recv()
                for c in key_core(s, src, False):
                    c.start()
        for cond, b in sides(d - 1):
            on(cond, functools.partial(process, b))

    gate_act = acc_g[...]
    hid[...] = (gate_act / (1.0 + jnp.exp(-gate_act)) * acc_u[...]).astype(jnp.bfloat16)
    for s in range(1, n_ep):
        gate_arrival(s).wait_recv()
    experts = gall.shape[1]
    mine = lax.broadcasted_iota(jnp.int32, (experts, 128), 0) == me

    for e in range(n_ep):
        row = jnp.sum(jnp.where(mine, gall[e], 0.0), axis=0, keepdims=True)
        square = jnp.broadcast_to(row, (128, 128)).T
        gcol[e * rows : (e + 1) * rows, :] = square[:rows, :]

    def cr(s, b):
        owner = x_of(s) * CORES + 1 - core
        return remote(part.at[b, owner], from_core.at[s, b], cr_send.at[s, b], cr_recv.at[s, b], ep=other)

    def xr(s, b):
        dst = x_of(s) * CORES + core
        return remote(part.at[b, dst], from_x.at[s - 1, b], xr_send.at[s, b], xr_recv.at[s, b], ep=dst)

    down_tile = 256 if width % 256 == 0 else 128

    def down(b):
        w_copies(b)[2].wait()

        def column(j, carry):
            cols = pl.ds(pl.multiple_of(j * down_tile, down_tile), down_tile)
            out = jnp.dot(hid[...], wd[b, :, cols], preferred_element_type=jnp.float32)
            out = (out * gcol[:, :1]).astype(jnp.bfloat16)
            part[b, :, :, cols] = out.reshape(n_ep, rows, down_tile)
            return carry

        lax.fori_loop(0, width // down_tile, column, 0)
        for s in range(1, n_x):
            cr(s, b).start()
        cr(0, b).start()

    def over_x(b):
        for s in range(1, n_x):
            dst = x_of(s) * CORES + core
            cr(s, b).wait_recv()
            part[b, dst] = (
                part[b, dst].astype(jnp.float32) + from_core[s, b].astype(jnp.float32)
            ).astype(jnp.bfloat16)
            xr(s, b).start()

    for d in range(n_tp - 1, -2, -1):
        now = sides(d) if d >= 0 else []
        before = sides(d + 1) if d + 1 < n_tp else []
        for cond, b in now[:1]:
            on(cond, functools.partial(down, b))
        for cond, b in before:
            on(cond, functools.partial(over_x, b))
        for cond, b in now[1:]:
            on(cond, functools.partial(down, b))

    for s in range(n_x):
        src = lax.rem(xx + n_x - s, n_x) * CORES + 1 - core
        for c in key_core(s, src, False):
            c.wait_recv()

    heads = ql_ref.shape[0] // rows
    rope = rots.shape[2]
    block_tokens = 16
    block = block_tokens * heads
    for e in range(n_ep):
        rope_keys[e * rows : (e + 1) * rows, :] = jnp.concatenate([rots[e]] * heads, axis=1)

    q_pos = me * rows + lax.broadcasted_iota(jnp.int32, (rows, tokens), 0)
    k_pos = lax.broadcasted_iota(jnp.int32, (rows, tokens), 1)
    q_prompt = jnp.zeros((rows, tokens), jnp.int32)
    k_prompt = jnp.zeros((rows, tokens), jnp.int32)
    end = jnp.int32(0)
    for doc in range(lengths_ref.shape[0]):
        end = end + lengths_ref[doc]
        q_prompt += (q_pos >= end).astype(jnp.int32)
        k_prompt += (k_pos >= end).astype(jnp.int32)
    hidden_from[...] = jnp.where((q_prompt == k_prompt) & (k_pos <= q_pos), 0.0, -1.0)

    spread_of = (block_tokens, heads, heads * rope)
    own_lanes = (
        lax.broadcasted_iota(jnp.int32, spread_of, 2) // rope == lax.broadcasted_iota(jnp.int32, spread_of, 1)
    )

    def attend(i, carry):
        at = pl.multiple_of(i * block, block)
        token_at = pl.ds(pl.multiple_of(i * block_tokens, block_tokens), block_tokens)
        all_keys = keys[...].reshape(tokens, keys.shape[2])
        dims = (((1,), (1,)), ((), ()))
        rotary = jnp.broadcast_to(qr_ref[token_at, :].astype(jnp.float32)[:, None, :], spread_of)
        rotary = jnp.where(own_lanes, rotary, 0.0).reshape(block, heads * rope).astype(jnp.bfloat16)
        scores = lax.dot_general(
            ql_ref[pl.ds(at, block), :], all_keys, dims, preferred_element_type=jnp.float32
        )
        scores += lax.dot_general(rotary, rope_keys[...], dims, preferred_element_type=jnp.float32)
        bias = hidden_from[token_at, :]
        bias = jnp.broadcast_to(bias[:, None, :], (block_tokens, heads, tokens)).reshape(block, tokens)
        masked = jnp.where(bias < 0.0, -1e30, scores * score_scale)
        top = jnp.max(masked, axis=1, keepdims=True)
        weights = jnp.where(bias < 0.0, 0.0, jnp.exp(masked - top))
        total = jnp.sum(weights, axis=1, keepdims=True)
        out = jnp.dot(weights.astype(jnp.bfloat16), all_keys, preferred_element_type=jnp.float32)
        ctx_ref[pl.ds(at, block), :] = (out / total).astype(jnp.bfloat16)
        return carry

    lax.fori_loop(0, rows // block_tokens, attend, 0)

    def zr(direction, b):
        to = z + 1 if direction == 0 else z - 1
        return remote(
            part.at[b, me], from_z.at[direction, b], zr_send.at[b], zr_recv.at[direction, b], tp=to
        )

    def chip_sum(b):
        cr(0, b).wait_recv()
        total = part[b, me].astype(jnp.float32) + from_core[0, b].astype(jnp.float32)
        for s in range(1, n_x):
            xr(s, b).wait_recv()
            total += from_x[s - 1, b].astype(jnp.float32)
        return total

    def along(direction, b, first):
        @pl.when(first)
        def _():
            part[b, me] = chip_sum(b).astype(jnp.bfloat16)

        @pl.when(jnp.logical_not(first))
        def _():
            zr(direction, b).wait_recv()
            part[b, me] = (chip_sum(b) + from_z[direction, b].astype(jnp.float32)).astype(jnp.bfloat16)

        zr(direction, b).start()

    for d in range(n_tp - 1, 0, -1):
        pl.when(z >= d)(functools.partial(along, 1, z - d, z == n_tp - 1))
        pl.when(z + d < n_tp)(functools.partial(along, 0, z + d, z == 0))

    zsum = acc_final = chip_sum(z)

    @pl.when(z == 0)
    def _():
        zr(1, z).wait_recv()
        moe_ref[...] = (acc_final + from_z[1, z].astype(jnp.float32)).astype(jnp.bfloat16)

    @pl.when(z == n_tp - 1)
    def _():
        zr(0, z).wait_recv()
        moe_ref[...] = (acc_final + from_z[0, z].astype(jnp.float32)).astype(jnp.bfloat16)

    @pl.when((z > 0) & (z < n_tp - 1))
    def _():
        zr(0, z).wait_recv()
        zr(1, z).wait_recv()
        moe_ref[...] = (
            zsum + from_z[0, z].astype(jnp.float32) + from_z[1, z].astype(jnp.float32)
        ).astype(jnp.bfloat16)

    for s in range(1, n_ep):
        gate_copy(s).wait_send()
    for s in range(1, n_x):
        for c in key_x(s):
            c.wait_send()
    for s in range(n_x):
        for c in key_core(s, me, True):
            c.wait_send()

    def drain(b, own):
        for s in range(1, n_x):
            xg(s, b, own).wait_send()
            xr(s, b).wait_send()
        for s in range(n_x):
            cg(s, b, me, False).wait_send()
            cr(s, b).wait_send()

    for d in range(n_tp):
        for cond, b in sides(d):
            on(cond, functools.partial(drain, b, d == 0))

    @pl.when(z < n_tp - 1)
    def _():
        zg(0, z, True).wait_send()

    @pl.when(z > 0)
    def _():
        zg(1, z, True).wait_send()

    for d in range(1, n_tp):

        @pl.when((z >= d) & (z < n_tp - 1))
        def _():
            zg(0, z - d, False).wait_send()

        @pl.when((z + d < n_tp) & (z > 0))
        def _():
            zg(1, z + d, False).wait_send()

        @pl.when(z >= d)
        def _():
            zr(1, z - d).wait_send()

        @pl.when(z + d < n_tp)
        def _():
            zr(0, z + d).wait_send()


def body(
    x_moe,
    routes,
    router_logits,
    w_gate,
    w_up,
    w_down,
    q_latent,
    q_rope,
    kv_latent,
    key_rope,
    prompt_lengths,
):
    n_ep = lax.axis_size("ep")
    n_tp = lax.axis_size("tp")
    n_x = n_ep // CORES
    rows, width = x_moe.shape
    _, heads, latent = q_latent.shape
    rope = key_rope.shape[1]
    units = w_gate.shape[2]
    tokens = n_ep * rows
    experts = max(8, n_ep)

    vmem = pl.BlockSpec(memory_space=pltpu.VMEM)
    smem = pl.BlockSpec(memory_space=pltpu.SMEM)
    hbm = pl.BlockSpec(memory_space=pl.ANY)
    bf16, f32 = jnp.bfloat16, jnp.float32
    dma = pltpu.SemaphoreType.DMA
    moe, ctx = pl.pallas_call(
        functools.partial(kernel, n_ep, n_tp),
        out_shape=(
            jax.ShapeDtypeStruct((rows, width), bf16),
            jax.ShapeDtypeStruct((rows * heads, latent), bf16),
        ),
        in_specs=[vmem] * 7 + [smem] + [hbm] * 3,
        out_specs=(vmem, vmem),
        scratch_shapes=[
            pltpu.VMEM((n_tp, n_ep, rows, width), bf16),
            pltpu.VMEM((experts, 128), f32),
            pltpu.VMEM((n_ep, experts, 128), f32),
            pltpu.VMEM((tokens, heads * rope), bf16),
            pltpu.VMEM((rows, tokens), f32),
            pltpu.VMEM((n_ep, rows, latent), bf16),
            pltpu.VMEM((n_ep, rows, rope), bf16),
            pltpu.VMEM((n_tp * width, units), bf16),
            pltpu.VMEM((n_tp * width, units), bf16),
            pltpu.VMEM((n_tp, units, width), bf16),
            pltpu.VMEM((tokens, units), f32),
            pltpu.VMEM((tokens, units), f32),
            pltpu.VMEM((tokens, units), bf16),
            pltpu.VMEM((tokens, 128), f32),
            pltpu.VMEM((n_tp, n_ep, rows, width), bf16),
            pltpu.VMEM((n_x, n_tp, rows, width), bf16),
            pltpu.VMEM((n_x - 1, n_tp, rows, width), bf16),
            pltpu.VMEM((2, n_tp, rows, width), bf16),
            dma((3, n_tp)),
            dma((5, n_ep)),
            dma((5, n_ep)),
            dma((2, n_tp)),
            dma((2, n_tp)),
            dma((n_x, n_tp)),
            dma((n_x, n_tp)),
            dma((n_x, n_tp)),
            dma((n_x, n_tp)),
            dma((n_x, n_tp)),
            dma((n_x, n_tp)),
            dma((n_x, n_tp)),
            dma((n_x, n_tp)),
            dma((n_tp,)),
            dma((2, n_tp)),
        ],
        compiler_params=pltpu.CompilerParams(
            collective_id=0, has_side_effects=True, vmem_limit_bytes=62 * 1024 * 1024
        ),
        name="layer",
    )(
        x_moe,
        routes,
        router_logits,
        q_latent.reshape(rows * heads, latent),
        q_rope,
        kv_latent,
        key_rope,
        prompt_lengths,
        w_gate,
        w_up,
        w_down,
    )
    return moe, ctx.reshape(rows, heads, latent)


def solution(mesh):
    in_specs = (
        P(("groups", "ep"), "tp"),
        P(("groups", "ep"), None),
        P(("groups", "ep"), None),
        P("ep", None, "tp"),
        P("ep", None, "tp"),
        P("ep", "tp", None),
        P(("groups", "ep"), "tp", None),
        P(("groups", "ep"), "tp"),
        P(("groups", "ep"), None),
        P(("groups", "ep"), None),
        P("groups"),
    )
    out_specs = (P(("groups", "ep"), "tp"), P(("groups", "ep"), "tp", None))
    return jax.shard_map(body, mesh=mesh, in_specs=in_specs, out_specs=out_specs, check_vma=False)
```

```python
import functools

import jax
import jax.numpy as jnp
from jax import lax
from jax.experimental import pallas as pl
from jax.experimental.pallas import tpu as pltpu
from jax.sharding import PartitionSpec as P

MESH = pl.DeviceIdType.MESH
score_scale = 192.0 ** (-0.5)
route_scale = 2.5
CORES = 2


def kernel(
    n_ep,
    n_tp,
    x_ref,
    routes_ref,
    logits_ref,
    ql_ref,
    qr_ref,
    kv_ref,
    kr_ref,
    lengths_ref,
    wg_ref,
    wu_ref,
    wd_ref,
    moe_ref,
    ctx_ref,
    xall,
    gt_ref,
    gall,
    rope_keys,
    hidden_from,
    keys,
    rots,
    wg,
    wu,
    wd,
    acc_g,
    acc_u,
    hid,
    gcol,
    part,
    from_core,
    from_x,
    from_z,
    w_sem,
    small_send,
    small_recv,
    zg_send,
    zg_recv,
    xg_send,
    xg_recv,
    cg_send,
    cg_recv,
    cr_send,
    cr_recv,
    xr_send,
    xr_recv,
    zr_send,
    zr_recv,
):
    n_x = n_ep // CORES
    me = lax.axis_index("ep")
    z = lax.axis_index("tp")
    core = me % CORES
    xx = me // CORES
    other = me + 1 - 2 * core
    rows, width = x_ref.shape
    hidden_units = wg.shape[1]
    tokens = n_ep * rows

    def remote(src, dst, send, recv, ep=None, tp=None):
        where = {}
        if ep is not None:
            where["ep"] = ep
        if tp is not None:
            where["tp"] = tp
        return pltpu.make_async_remote_copy(
            src_ref=src, dst_ref=dst, send_sem=send, recv_sem=recv, device_id=where, device_id_type=MESH
        )

    def ep_peer(step):
        return lax.rem(me + step, n_ep)

    def x_of(step):
        return lax.rem(xx + step, n_x)

    def w_copies(b):
        span = pl.ds(pl.multiple_of(b * width, width), width)
        return (
            pltpu.make_async_copy(wg_ref.at[0, span, :], wg.at[span, :], w_sem.at[0, b]),
            pltpu.make_async_copy(wu_ref.at[0, span, :], wu.at[span, :], w_sem.at[1, b]),
            pltpu.make_async_copy(
                wd_ref.at[0, :, pl.ds(pl.multiple_of(b * width, 128), width)], wd.at[b], w_sem.at[2, b]
            ),
        )

    def sides(d):
        if d == 0:
            return [(None, z)]
        return [(z >= d, z - d), (z + d < n_tp, z + d)]

    def on(cond, fn):
        if cond is None:
            fn()
        else:
            pl.when(cond)(fn)

    def start_w(d, which):
        for cond, b in sides(d):

            def go(b=b):
                for i in which:
                    w_copies(b)[i].start()

            on(cond, go)

    barrier = pltpu.get_barrier_semaphore()
    for s in range(1, n_ep):
        pl.semaphore_signal(barrier, inc=1, device_id={"ep": ep_peer(s)}, device_id_type=MESH)

    @pl.when(z > 0)
    def _():
        pl.semaphore_signal(barrier, inc=1, device_id={"tp": z - 1}, device_id_type=MESH)

    @pl.when(z < n_tp - 1)
    def _():
        pl.semaphore_signal(barrier, inc=1, device_id={"tp": z + 1}, device_id_type=MESH)

    probs = 1.0 / (1.0 + jnp.exp(-logits_ref[...]))
    gates = route_scale * probs / jnp.sum(probs, axis=0, keepdims=True)
    names = lax.broadcasted_iota(jnp.int32, (gt_ref.shape[0], rows), 0)
    table = jnp.zeros((gt_ref.shape[0], rows), jnp.float32)
    for k in range(routes_ref.shape[0]):
        table += jnp.where(routes_ref[k : k + 1, :] == names, gates[k : k + 1, :], 0.0)
    gt_ref[...] = jnp.zeros_like(gt_ref)
    gt_ref[:, :rows] = table

    edge = (z == 0) | (z == n_tp - 1)

    @pl.when(edge)
    def _():
        pl.semaphore_wait(barrier, n_ep)

    @pl.when(jnp.logical_not(edge))
    def _():
        pl.semaphore_wait(barrier, n_ep + 1)

    def gate_copy(s):
        return remote(gt_ref, gall.at[me], small_send.at[0, s], small_recv.at[0, s], ep=ep_peer(s))

    def gate_arrival(s):
        src = lax.rem(me + n_ep - s, n_ep)
        return remote(gt_ref, gall.at[src], small_send.at[0, s], small_recv.at[0, s], ep=ep_peer(s))

    def key_x(s):
        dst = x_of(s) * CORES + core
        return (
            remote(kv_ref, keys.at[me], small_send.at[1, s], small_recv.at[1, s], ep=dst),
            remote(kr_ref, rots.at[me], small_send.at[2, s], small_recv.at[2, s], ep=dst),
        )

    def key_core(s, owner, own):
        src_kv = kv_ref if own else keys.at[owner]
        src_kr = kr_ref if own else rots.at[owner]
        return (
            remote(src_kv, keys.at[owner], small_send.at[3, s], small_recv.at[3, s], ep=other),
            remote(src_kr, rots.at[owner], small_send.at[4, s], small_recv.at[4, s], ep=other),
        )

    def zg(direction, b, own):
        to = z + 1 if direction == 0 else z - 1
        return remote(
            x_ref if own else xall.at[b, me],
            xall.at[b, me],
            zg_send.at[direction, b],
            zg_recv.at[direction, b],
            tp=to,
        )

    def xg(s, b, own):
        return remote(
            x_ref if own else xall.at[b, me],
            xall.at[b, me],
            xg_send.at[s, b],
            xg_recv.at[s, b],
            ep=x_of(s) * CORES + core,
        )

    def xg_in(s, b):
        src = lax.rem(xx + n_x - s, n_x) * CORES + core
        return remote(xall.at[b, src], xall.at[b, src], xg_send.at[s, b], xg_recv.at[s, b], ep=src), src

    def cg(s, b, owner, own):
        return remote(
            x_ref if own else xall.at[b, owner],
            xall.at[b, owner],
            cg_send.at[s, b],
            cg_recv.at[s, b],
            ep=other,
        )

    def cg_in(s, b):
        src = lax.rem(xx + n_x - s, n_x) * CORES + 1 - core
        return remote(xall.at[b, src], xall.at[b, src], cg_send.at[s, b], cg_recv.at[s, b], ep=other)

    def spread(b, own):
        for s in range(1, n_x):
            xg(s, b, own).start()
        cg(0, b, me, own).start()

    @pl.when(z < n_tp - 1)
    def _():
        zg(0, z, True).start()

    @pl.when(z > 0)
    def _():
        zg(1, z, True).start()

    spread(z, True)
    for s in range(1, n_x):
        for c in key_x(s):
            c.start()
    for c in key_core(0, me, True):
        c.start()
    for s in range(1, n_ep):
        gate_copy(s).start()

    for d in range(n_tp):
        start_w(d, (0, 1))
    xall[z, me] = x_ref[...]
    keys[me] = kv_ref[...]
    rots[me] = kr_ref[...]
    gall[me] = gt_ref[...]
    acc_g[...] = jnp.zeros_like(acc_g)
    acc_u[...] = jnp.zeros_like(acc_u)


    tile = 256

    def multiply(b):
        for i in (0, 1):
            w_copies(b)[i].wait()
        span = pl.ds(pl.multiple_of(b * width, width), width)

        def column(j, carry):
            cols = pl.ds(pl.multiple_of(j * tile, tile), tile)
            x = xall[b].reshape(tokens, width)
            acc_g[:, cols] += jnp.dot(x, wg[span, cols], preferred_element_type=jnp.float32)
            acc_u[:, cols] += jnp.dot(x, wu[span, cols], preferred_element_type=jnp.float32)
            return carry

        lax.fori_loop(0, hidden_units // tile, column, 0)

    def process(b):
        for s in range(1, n_x):
            arrival, src = xg_in(s, b)
            arrival.wait_recv()
            cg(s, b, src, False).start()
        for s in range(n_x):
            cg_in(s, b).wait_recv()
        multiply(b)

    for d in range(1, n_tp + 1):
        if d < n_tp:

            @pl.when(z >= d)
            def _():
                b = z - d
                zg(0, b, False).wait_recv()

                @pl.when(z < n_tp - 1)
                def _():
                    zg(0, b, False).start()

                spread(b, False)

            @pl.when(z + d < n_tp)
            def _():
                b = z + d
                zg(1, b, False).wait_recv()

                @pl.when(z > 0)
                def _():
                    zg(1, b, False).start()

                spread(b, False)

        if d == 2:
            for far in range(n_tp - 1, -1, -1):
                start_w(far, (2,))
            for s in range(1, n_x):
                src = lax.rem(xx + n_x - s, n_x) * CORES + core
                for c in key_x(s):
                    c.wait_recv()
                for c in key_core(s, src, False):
                    c.start()
        for cond, b in sides(d - 1):
            on(cond, functools.partial(process, b))

    gate_act = acc_g[...]
    hid[...] = (gate_act / (1.0 + jnp.exp(-gate_act)) * acc_u[...]).astype(jnp.bfloat16)
    for s in range(1, n_ep):
        gate_arrival(s).wait_recv()
    experts = gall.shape[1]
    mine = lax.broadcasted_iota(jnp.int32, (experts, 128), 0) == me

    for e in range(n_ep):
        row = jnp.sum(jnp.where(mine, gall[e], 0.0), axis=0, keepdims=True)
        square = jnp.broadcast_to(row, (128, 128)).T
        gcol[e * rows : (e + 1) * rows, :] = square[:rows, :]

    def cr(s, b):
        owner = x_of(s) * CORES + 1 - core
        return remote(part.at[b, owner], from_core.at[s, b], cr_send.at[s, b], cr_recv.at[s, b], ep=other)

    def xr(s, b):
        dst = x_of(s) * CORES + core
        return remote(part.at[b, dst], from_x.at[s - 1, b], xr_send.at[s, b], xr_recv.at[s, b], ep=dst)

    down_tile = 256 if width % 256 == 0 else 128

    def down(b):
        w_copies(b)[2].wait()

        def column(j, carry):
            cols = pl.ds(pl.multiple_of(j * down_tile, down_tile), down_tile)
            out = jnp.dot(hid[...], wd[b, :, cols], preferred_element_type=jnp.float32)
            out = (out * gcol[:, :1]).astype(jnp.bfloat16)
            part[b, :, :, cols] = out.reshape(n_ep, rows, down_tile)
            return carry

        lax.fori_loop(0, width // down_tile, column, 0)
        for s in range(1, n_x):
            cr(s, b).start()
        cr(0, b).start()

    def over_x(b):
        for s in range(1, n_x):
            dst = x_of(s) * CORES + core
            cr(s, b).wait_recv()
            part[b, dst] = (
                part[b, dst].astype(jnp.float32) + from_core[s, b].astype(jnp.float32)
            ).astype(jnp.bfloat16)
            xr(s, b).start()

    for d in range(n_tp - 1, -2, -1):
        now = sides(d) if d >= 0 else []
        before = sides(d + 1) if d + 1 < n_tp else []
        for cond, b in now[:1]:
            on(cond, functools.partial(down, b))
        for cond, b in before:
            on(cond, functools.partial(over_x, b))
        for cond, b in now[1:]:
            on(cond, functools.partial(down, b))

    for s in range(n_x):
        src = lax.rem(xx + n_x - s, n_x) * CORES + 1 - core
        for c in key_core(s, src, False):
            c.wait_recv()

    heads = ql_ref.shape[0] // rows
    rope = rots.shape[2]
    block_tokens = 16
    block = block_tokens * heads
    for e in range(n_ep):
        rope_keys[e * rows : (e + 1) * rows, :] = jnp.concatenate([rots[e]] * heads, axis=1)

    q_pos = me * rows + lax.broadcasted_iota(jnp.int32, (rows, tokens), 0)
    k_pos = lax.broadcasted_iota(jnp.int32, (rows, tokens), 1)
    q_prompt = jnp.zeros((rows, tokens), jnp.int32)
    k_prompt = jnp.zeros((rows, tokens), jnp.int32)
    end = jnp.int32(0)
    for doc in range(lengths_ref.shape[0]):
        end = end + lengths_ref[doc]
        q_prompt += (q_pos >= end).astype(jnp.int32)
        k_prompt += (k_pos >= end).astype(jnp.int32)
    hidden_from[...] = jnp.where((q_prompt == k_prompt) & (k_pos <= q_pos), 0.0, -1.0)

    spread_of = (block_tokens, heads, heads * rope)
    own_lanes = (
        lax.broadcasted_iota(jnp.int32, spread_of, 2) // rope == lax.broadcasted_iota(jnp.int32, spread_of, 1)
    )

    def attend(i, carry):
        at = pl.multiple_of(i * block, block)
        token_at = pl.ds(pl.multiple_of(i * block_tokens, block_tokens), block_tokens)
        all_keys = keys[...].reshape(tokens, keys.shape[2])
        dims = (((1,), (1,)), ((), ()))
        rotary = jnp.broadcast_to(qr_ref[token_at, :].astype(jnp.float32)[:, None, :], spread_of)
        rotary = jnp.where(own_lanes, rotary, 0.0).reshape(block, heads * rope).astype(jnp.bfloat16)
        scores = lax.dot_general(
            ql_ref[pl.ds(at, block), :], all_keys, dims, preferred_element_type=jnp.float32
        )
        scores += lax.dot_general(rotary, rope_keys[...], dims, preferred_element_type=jnp.float32)
        bias = hidden_from[token_at, :]
        bias = jnp.broadcast_to(bias[:, None, :], (block_tokens, heads, tokens)).reshape(block, tokens)
        masked = jnp.where(bias < 0.0, -1e30, scores * score_scale)
        top = jnp.max(masked, axis=1, keepdims=True)
        weights = jnp.where(bias < 0.0, 0.0, jnp.exp(masked - top))
        total = jnp.sum(weights, axis=1, keepdims=True)
        out = jnp.dot(weights.astype(jnp.bfloat16), all_keys, preferred_element_type=jnp.float32)
        ctx_ref[pl.ds(at, block), :] = (out / total).astype(jnp.bfloat16)
        return carry

    lax.fori_loop(0, rows // block_tokens, attend, 0)

    def zr(direction, b):
        to = z + 1 if direction == 0 else z - 1
        return remote(
            part.at[b, me], from_z.at[direction, b], zr_send.at[b], zr_recv.at[direction, b], tp=to
        )

    def chip_sum(b):
        cr(0, b).wait_recv()
        total = part[b, me].astype(jnp.float32) + from_core[0, b].astype(jnp.float32)
        for s in range(1, n_x):
            xr(s, b).wait_recv()
            total += from_x[s - 1, b].astype(jnp.float32)
        return total

    def along(direction, b, first):
        @pl.when(first)
        def _():
            part[b, me] = chip_sum(b).astype(jnp.bfloat16)

        @pl.when(jnp.logical_not(first))
        def _():
            zr(direction, b).wait_recv()
            part[b, me] = (chip_sum(b) + from_z[direction, b].astype(jnp.float32)).astype(jnp.bfloat16)

        zr(direction, b).start()

    for d in range(n_tp - 1, 0, -1):
        pl.when(z >= d)(functools.partial(along, 1, z - d, z == n_tp - 1))
        pl.when(z + d < n_tp)(functools.partial(along, 0, z + d, z == 0))

    zsum = acc_final = chip_sum(z)

    @pl.when(z == 0)
    def _():
        zr(1, z).wait_recv()
        moe_ref[...] = (acc_final + from_z[1, z].astype(jnp.float32)).astype(jnp.bfloat16)

    @pl.when(z == n_tp - 1)
    def _():
        zr(0, z).wait_recv()
        moe_ref[...] = (acc_final + from_z[0, z].astype(jnp.float32)).astype(jnp.bfloat16)

    @pl.when((z > 0) & (z < n_tp - 1))
    def _():
        zr(0, z).wait_recv()
        zr(1, z).wait_recv()
        moe_ref[...] = (
            zsum + from_z[0, z].astype(jnp.float32) + from_z[1, z].astype(jnp.float32)
        ).astype(jnp.bfloat16)

    for s in range(1, n_ep):
        gate_copy(s).wait_send()
    for s in range(1, n_x):
        for c in key_x(s):
            c.wait_send()
    for s in range(n_x):
        for c in key_core(s, me, True):
            c.wait_send()

    def drain(b, own):
        for s in range(1, n_x):
            xg(s, b, own).wait_send()
            xr(s, b).wait_send()
        for s in range(n_x):
            cg(s, b, me, False).wait_send()
            cr(s, b).wait_send()

    for d in range(n_tp):
        for cond, b in sides(d):
            on(cond, functools.partial(drain, b, d == 0))

    @pl.when(z < n_tp - 1)
    def _():
        zg(0, z, True).wait_send()

    @pl.when(z > 0)
    def _():
        zg(1, z, True).wait_send()

    for d in range(1, n_tp):

        @pl.when((z >= d) & (z < n_tp - 1))
        def _():
            zg(0, z - d, False).wait_send()

        @pl.when((z + d < n_tp) & (z > 0))
        def _():
            zg(1, z + d, False).wait_send()

        @pl.when(z >= d)
        def _():
            zr(1, z - d).wait_send()

        @pl.when(z + d < n_tp)
        def _():
            zr(0, z + d).wait_send()


def body(
    x_moe,
    routes,
    router_logits,
    w_gate,
    w_up,
    w_down,
    q_latent,
    q_rope,
    kv_latent,
    key_rope,
    prompt_lengths,
):
    n_ep = lax.axis_size("ep")
    n_tp = lax.axis_size("tp")
    n_x = n_ep // CORES
    rows, width = x_moe.shape
    _, heads, latent = q_latent.shape
    rope = key_rope.shape[1]
    units = w_gate.shape[2]
    tokens = n_ep * rows
    experts = max(8, n_ep)

    vmem = pl.BlockSpec(memory_space=pltpu.VMEM)
    smem = pl.BlockSpec(memory_space=pltpu.SMEM)
    hbm = pl.BlockSpec(memory_space=pl.ANY)
    bf16, f32 = jnp.bfloat16, jnp.float32
    dma = pltpu.SemaphoreType.DMA
    moe, ctx = pl.pallas_call(
        functools.partial(kernel, n_ep, n_tp),
        out_shape=(
            jax.ShapeDtypeStruct((rows, width), bf16),
            jax.ShapeDtypeStruct((rows * heads, latent), bf16),
        ),
        in_specs=[vmem] * 7 + [smem] + [hbm] * 3,
        out_specs=(vmem, vmem),
        scratch_shapes=[
            pltpu.VMEM((n_tp, n_ep, rows, width), bf16),
            pltpu.VMEM((experts, 128), f32),
            pltpu.VMEM((n_ep, experts, 128), f32),
            pltpu.VMEM((tokens, heads * rope), bf16),
            pltpu.VMEM((rows, tokens), f32),
            pltpu.VMEM((n_ep, rows, latent), bf16),
            pltpu.VMEM((n_ep, rows, rope), bf16),
            pltpu.VMEM((n_tp * width, units), bf16),
            pltpu.VMEM((n_tp * width, units), bf16),
            pltpu.VMEM((n_tp, units, width), bf16),
            pltpu.VMEM((tokens, units), f32),
            pltpu.VMEM((tokens, units), f32),
            pltpu.VMEM((tokens, units), bf16),
            pltpu.VMEM((tokens, 128), f32),
            pltpu.VMEM((n_tp, n_ep, rows, width), bf16),
            pltpu.VMEM((n_x, n_tp, rows, width), bf16),
            pltpu.VMEM((n_x - 1, n_tp, rows, width), bf16),
            pltpu.VMEM((2, n_tp, rows, width), bf16),
            dma((3, n_tp)),
            dma((5, n_ep)),
            dma((5, n_ep)),
            dma((2, n_tp)),
            dma((2, n_tp)),
            dma((n_x, n_tp)),
            dma((n_x, n_tp)),
            dma((n_x, n_tp)),
            dma((n_x, n_tp)),
            dma((n_x, n_tp)),
            dma((n_x, n_tp)),
            dma((n_x, n_tp)),
            dma((n_x, n_tp)),
            dma((n_tp,)),
            dma((2, n_tp)),
        ],
        compiler_params=pltpu.CompilerParams(
            collective_id=0, has_side_effects=True, vmem_limit_bytes=62 * 1024 * 1024
        ),
        name="layer",
    )(
        x_moe,
        routes.T,
        router_logits.T,
        q_latent.reshape(rows * heads, latent),
        q_rope,
        kv_latent,
        key_rope,
        prompt_lengths,
        w_gate,
        w_up,
        w_down,
    )
    return moe, ctx.reshape(rows, heads, latent)


def solution(mesh):
    in_specs = (
        P(("groups", "ep"), "tp"),
        P(("groups", "ep"), None),
        P(("groups", "ep"), None),
        P("ep", None, "tp"),
        P("ep", None, "tp"),
        P("ep", "tp", None),
        P(("groups", "ep"), "tp", None),
        P(("groups", "ep"), "tp"),
        P(("groups", "ep"), None),
        P(("groups", "ep"), None),
        P("groups"),
    )
    out_specs = (P(("groups", "ep"), "tp"), P(("groups", "ep"), "tp", None))
    return jax.shard_map(body, mesh=mesh, in_specs=in_specs, out_specs=out_specs, check_vma=False)
```
